128 devices in a mesh: ctx: 8 (over y, x_hi), head: 16 (over z, x_lo, core).
Axes of the slice: x: 4 (x_hi: 2, x_lo: 2; x = x_hi * 2 + x_lo), y: 4, z: 4, core: 2. Of those that a mesh axis runs over, the one named last changes fastest.
Arguments:
- queries: bfloat16 [4096, 8192], P('ctx', 'head'), may hold values from -8 to 8
- prefix_kv: bfloat16 [16, 8192, 128], P('head', 'ctx'), may hold values from -8 to 8
- cand_kv: bfloat16 [16, 4096, 128], P('head', 'ctx'), may hold values from -8 to 8
- lengths: int32 [64], P('ctx'), may hold values from 1 to 64, 3072 in all
- out_weight: bfloat16 [8192, 8192], P(None, 'head'), may hold values from -0.0625 to 0.0625
Outputs:
- mixed: bfloat16 [4096, 8192], P('ctx', 'head')
The draws below stay inside these ranges and needn't reach their ends.
Inputs may be any that keep to these rules, and one draw needn't show every extreme that they name: `lengths`: each candidate has at least one live token; some candidate has all 64 live.
All inputs are finite; a program needn't handle non-finite values. No bound on the sum of `lengths` on one device may be relied on, other than what follows from the above.
Results may differ from the reference program's by a relative error of at most 0.012.
Values may be sent and summed in bfloat16 or wider, within the bound.
A program may use at most 192 MiB of HBM per device.

```python
import math
import jax
import jax.numpy as jnp
import numpy as np
from jax import lax

D = 8192
H = 64
KVH = 8
HD = 128
STEP_TOK = 64
CANDS = 64
CAND_TOK = 4096
PREFIX = 8192


def shared_direction(key):
    return jax.random.normal(jax.random.fold_in(key, 21), (CAND_TOK, KVH, HD), jnp.float32)


def draw_prefix_kv(key, part):
    key = jax.random.fold_in(key, 11)
    key_noise, key_means = jax.random.split(key)
    noise = jax.random.normal(key_noise, (KVH, 2, PREFIX, HD), jnp.float32)
    region_index = jnp.arange(PREFIX) * 8 // PREFIX
    region_means = jax.random.normal(key_means, (KVH, 8, HD), jnp.float32)
    value_rows = noise[:, 1] + region_means[:, region_index, :]
    key_rows = noise[:, 0]
    stacked = jnp.stack([key_rows, value_rows], axis=1)
    return jnp.clip(stacked, -8.0, 8.0).reshape(2 * KVH, PREFIX, HD).astype(jnp.bfloat16)


def draw_cand_kv(key, part):
    direction = shared_direction(key)
    key = jax.random.fold_in(key, 13)
    noise = jax.random.normal(key, (KVH, 2, CAND_TOK, HD), jnp.float32)
    key_rows = 0.9 * direction.transpose(1, 0, 2) + 0.44 * noise[:, 0]
    value_rows = noise[:, 1]
    stacked = jnp.stack([key_rows, value_rows], axis=1)
    return jnp.clip(stacked, -8.0, 8.0).reshape(2 * KVH, CAND_TOK, HD).astype(jnp.bfloat16)


def draw_queries(key, part):
    direction = shared_direction(key)
    key = jax.random.fold_in(key, 12)
    head_ids = jnp.arange(H)
    common = direction[:, head_ids // (H // KVH), :].reshape(CAND_TOK, H * HD)
    noise = jax.random.normal(key, (CAND_TOK, H * HD), jnp.float32)
    noise = 0.8 * common + 0.6 * noise
    return jnp.clip(noise, -8.0, 8.0).astype(jnp.bfloat16)


def steps_of(rng, dims, shards, least, largest):
    gain = 1.0
    for axis_at, blocks in shards:
        heights = jax.random.uniform(jax.random.fold_in(jax.random.fold_in(rng, 6), axis_at), (blocks,), jnp.float32, least / len(shards), largest / len(shards))
        gain = gain * jnp.repeat(jnp.exp(heights), dims[axis_at] // blocks).reshape((-1,) + (1,) * (len(dims) - 1 - axis_at))
    return gain


def split_up(amount, total, limit, lean):
    weights = [(1 << 20) // math.isqrt(standing ** lean) + 1 for standing in range(2, amount + 1)]
    spare, holding = total - limit - (amount - 1), [1] * (amount - 1)
    while spare > 0:
        free = [i for i in range(amount - 1) if holding[i] < limit]
        whole, remaining = sum([weights[i] for i in free]), spare
        for i in free:
            addition = min(limit - holding[i], max(1, remaining * weights[i] // whole), spare)
            holding[i] = holding[i] + addition
            spare = spare - addition
    return np.array([limit] + holding)


def uneven_parts(own_key, number_of, total, reach, skew):
    if number_of == 2:
        one = jax.random.randint(own_key, (), max(1, total - reach), min(reach, total - 1) + 1)
        return jnp.stack([one, total - one])
    sizes = jnp.asarray(split_up(number_of, total, reach, skew), jnp.int32)
    pairs = (number_of - 1) // 2
    donor, receiver = sizes[1:1 + 2 * pairs:2], sizes[2:2 + 2 * pairs:2]
    room = jnp.minimum(donor - 1, reach - receiver)
    shifted = jax.random.randint(jax.random.fold_in(own_key, 1), (pairs,), 0, 1 << 20) % (room + 1)
    sizes = sizes.at[1:1 + 2 * pairs:2].set(donor - shifted).at[2:2 + 2 * pairs:2].set(receiver + shifted)
    return sizes[jax.random.permutation(jax.random.fold_in(own_key, 2), number_of)]


def centred(key, dims, spread, reach, pieces=(), kind=jnp.bfloat16):
    array = jax.random.normal(key, dims, jnp.float32) * spread
    if len(pieces) > 0:
        array = steps_of(key, dims, pieces, -0.22, 0.18) * array
    return jnp.clip(array, min=-reach, max=reach).astype(kind)


def setup_inputs(seed: int = 0) -> dict:
    key_list = jax.random.split(jax.random.key(seed), 6)
    return {
        "queries": draw_queries(jax.random.fold_in(key_list[5], 71), 0),
        "prefix_kv": draw_prefix_kv(jax.random.fold_in(key_list[5], 71), 0),
        "cand_kv": draw_cand_kv(jax.random.fold_in(key_list[5], 71), 0),
        "lengths": uneven_parts(key_list[3], CANDS, CANDS * STEP_TOK * 3 // 4, STEP_TOK, 0).astype(jnp.int32),
        "out_weight": centred(key_list[4], (H * HD, D), (H * HD) ** -0.5, 0.0625, ((1, 16),)),
    }


NEG_FILL = -1.0e30


def reference(queries, prefix_kv, cand_kv, lengths, out_weight):
    group_size = H // KVH
    score_scale = HD ** -0.5
    offsets = jnp.arange(STEP_TOK, dtype=jnp.int32)
    visible = (offsets[None, :] <= offsets[:, None])[None] & (offsets[None, None, :] < lengths[:, None, None])
    visible_rows = visible.reshape(CAND_TOK, STEP_TOK)

    def one_head(head_index):
        kv_index = (2 * (head_index // group_size)).astype(jnp.int32)
        query_cols = lax.dynamic_slice_in_dim(queries, (head_index * HD).astype(jnp.int32), HD, 1)
        pre_keys = lax.dynamic_index_in_dim(prefix_kv, kv_index, 0, False)
        pre_vals = lax.dynamic_index_in_dim(prefix_kv, kv_index + 1, 0, False)
        suffix_keys = lax.dynamic_index_in_dim(cand_kv, kv_index, 0, False)
        suffix_vals = lax.dynamic_index_in_dim(cand_kv, kv_index + 1, 0, False)
        prefix_scores = jnp.dot(query_cols, pre_keys.T, preferred_element_type=jnp.float32) * score_scale
        suffix_scores = jnp.einsum(
            'cth,csh->cts',
            query_cols.reshape(CANDS, STEP_TOK, HD).astype(jnp.float32),
            suffix_keys.reshape(CANDS, STEP_TOK, HD).astype(jnp.float32)) * score_scale
        suffix_scores = jnp.where(visible, suffix_scores, NEG_FILL).reshape(CAND_TOK, STEP_TOK)
        row_max = jnp.maximum(jnp.max(prefix_scores, axis=1), jnp.max(suffix_scores, axis=1))
        prefix_probs = jnp.exp(prefix_scores - row_max[:, None])
        suffix_probs = jnp.where(visible_rows, jnp.exp(suffix_scores - row_max[:, None]), 0.0)
        row_total = jnp.sum(prefix_probs, axis=1) + jnp.sum(suffix_probs, axis=1)
        rounded = lax.optimization_barrier(suffix_probs.astype(jnp.bfloat16)).astype(jnp.float32)
        numerator = jnp.dot(prefix_probs.astype(jnp.bfloat16), pre_vals, preferred_element_type=jnp.float32)
        numerator = numerator + jnp.einsum(
            'cts,csh->cth',
            rounded.reshape(CANDS, STEP_TOK, STEP_TOK),
            suffix_vals.reshape(CANDS, STEP_TOK, HD).astype(jnp.float32)).reshape(CAND_TOK, HD)
        return (numerator / row_total[:, None]).astype(jnp.bfloat16)

    per_head = lax.map(one_head, jnp.arange(H, dtype=jnp.int32))
    attended = per_head.transpose(1, 0, 2).reshape(CAND_TOK, H * HD)
    return jnp.dot(attended, out_weight, preferred_element_type=jnp.float32).astype(jnp.bfloat16)
```

```python
import functools
import math

import jax
import jax.numpy as jnp
from jax import lax
from jax.experimental import pallas as pl
from jax.experimental.pallas import tpu as pltpu
from jax.sharding import PartitionSpec as P

MESH = pl.DeviceIdType.MESH
BF = jnp.bfloat16
F32 = jnp.float32
NEG_FILL = -1e30
NT = (((1,), (1,)), ((), ()))

FORWARD, BACK, ACROSS, OVER = 0, 1, 2, 3
KINDS = 15


def attend_kernel(
    lengths_ref, q_hbm, pre_hbm, cand_hbm, w_hbm, out_ref,
    kv, cand, q_raw, q_two, weights, acc, row_max, att, total,
    local_sem, cand_sem, s1, r1, b1, s2, r2, b2,
):
    ctx, head = lax.axis_index("ctx"), lax.axis_index("head")
    y, x_hi = ctx // 2, ctx % 2
    z, x_lo, core = head // 4, (head // 2) % 2, head % 2

    def ring1(d):
        return (lax.rem(y + d, 4) * 2 + x_hi, head)

    def ring2(d):
        return (ctx, lax.rem(z + d, 4) * 4 + x_lo * 2 + core)

    over1 = (y * 2 + 1 - x_hi, head)
    over2 = (ctx, z * 4 + (1 - x_lo) * 2 + core)
    sibling = (ctx, z * 4 + x_lo * 2 + 1 - core)
    near1 = {FORWARD: ring1(1), BACK: ring1(3), ACROSS: ring1(2), OVER: over1}
    near2 = {FORWARD: ring2(1), BACK: ring2(3), ACROSS: ring2(2), OVER: over2}

    barrier = pltpu.get_barrier_semaphore()
    others = [*near1.values(), *near2.values(), sibling]
    for other in others:
        pl.semaphore_signal(barrier, inc=1, device_id=other, device_id_type=MESH)

    local = [
        pltpu.make_async_copy(pre_hbm.at[0], kv.at[core, 0], local_sem.at[0]),
        pltpu.make_async_copy(cand_hbm.at[0], cand.at[core], local_sem.at[1]),
        pltpu.make_async_copy(q_hbm, q_raw, local_sem.at[2]),
        pltpu.make_async_copy(w_hbm, weights, local_sem.at[3]),
    ]
    for copy in local[:3]:
        copy.start()

    def remote(src, dst, send, recv, device):
        return pltpu.make_async_remote_copy(
            src_ref=src, dst_ref=dst, send_sem=send, recv_sem=recv, device_id=device, device_id_type=MESH
        )

    rows1 = kv.shape[2] // CHUNKS1

    def piece1(slot, c):
        return kv.at[core, slot, pl.ds(c * rows1, rows1)]

    def piece2(slot, c):
        return att.at[slot, core, c]

    sent = []

    def send(phase, src_slot, dst_slot, c, kind, device):
        piece, ss, rr = (piece1, s1, r1) if phase == 1 else (piece2, s2, r2)
        src = piece(src_slot, c)
        if phase == 1 and src_slot == 0:
            src = pre_hbm.at[0, pl.ds(c * rows1, rows1)]
        copy = remote(src, piece(dst_slot, c), ss.at[kind, c], rr.at[dst_slot, c], device)
        copy.start()
        sent.append(copy)

    def share(phase, slot, c):
        piece, ss, bb = (piece1, s1, b1) if phase == 1 else (piece2, s2, b2)
        src = piece(slot, c)
        if phase == 1 and slot == 0:
            src = pre_hbm.at[0, pl.ds(c * rows1, rows1)]
        copy = remote(src, piece(slot, c), ss.at[7 + slot, c], bb.at[slot, c], sibling)
        copy.start()
        sent.append(copy)

    def arrived(phase, slot, c):
        piece, rr = (piece1, r1) if phase == 1 else (piece2, r2)
        ref = piece(slot, c)
        remote(ref, ref, rr.at[slot, c], rr.at[slot, c], sibling).wait_recv()

    def shared(phase, slot, c):
        if phase == 1:
            ref, bb = kv.at[1 - core, slot, pl.ds(c * rows1, rows1)], b1
        else:
            ref, bb = att.at[slot, 1 - core, c], b2
        remote(ref, ref, bb.at[slot, c], bb.at[slot, c], sibling).wait_recv()

    def near(phase):
        return near1 if phase == 1 else near2

    def own_near(phase, c):
        n = near(phase)
        send(phase, 0, 1, c, 3, n[OVER])
        send(phase, 0, 3, c, 0, n[FORWARD])
        send(phase, 0, 2, c, 1, n[BACK])

    def own_far(phase, c):
        send(phase, 0, 4, c, 2, near(phase)[ACROSS])

    def on_partner(phase, c):
        arrived(phase, 1, c)
        n = near(phase)
        send(phase, 1, 6, c, 4, n[FORWARD])
        send(phase, 1, 5, c, 5, n[BACK])
        share(phase, 1, c)

    def on_far(phase, c):
        arrived(phase, 4, c)
        send(phase, 4, 7, c, 6, near(phase)[OVER])
        share(phase, 4, c)

    def on_plain(phase, slot, c):
        arrived(phase, slot, c)
        share(phase, slot, c)

    pl.semaphore_wait(barrier, len(others))

    cand_copy = remote(cand_hbm.at[0], cand.at[core], cand_sem.at[0], cand_sem.at[1], sibling)
    cand_copy.start()
    for c in range(CHUNKS1):
        own_near(1, c)
    for c in range(CHUNKS1):
        share(1, 0, c)
    for c in range(CHUNKS1):
        own_far(1, c)
    local[3].start()

    heads = q_two.shape[0]
    hd = kv.shape[3]
    factor = hd ** (-0.5) * math.log2(math.e)
    local[2].wait()
    for h in range(heads):
        scaled = q_raw[:, h * hd : (h + 1) * hd].astype(F32) * factor
        high = scaled.astype(BF)
        q_two[h, :, :hd] = high
        q_two[h, :, hd:] = (scaled - high.astype(F32)).astype(BF)

    tokens = q_two.shape[1]
    half = tokens // 2
    pairs = [(h, r) for h in range(heads) for r in (0, half)]

    def twice(k):
        return jnp.concatenate([k, k], axis=1)

    def with_ones(v):
        return jnp.concatenate([v, jnp.ones_like(v)], axis=1)

    def scores(h, r, keys):
        return lax.dot_general(q_two[h, r : r + half], twice(keys), NT, preferred_element_type=F32)

    def ahead(units, first, second):
        held = first(*units[0])
        for i, unit in enumerate(units):
            following = first(*units[i + 1]) if i + 1 < len(units) else None
            second(held, *unit)
            held = following

    local[1].wait()
    remote(cand.at[1 - core], cand.at[1 - core], cand_sem.at[0], cand_sem.at[1], sibling).wait_recv()
    slots = tokens // lengths_ref.shape[0]
    per = half // slots
    row = lax.broadcasted_iota(jnp.int32, (half, half), 0)
    col = lax.broadcasted_iota(jnp.int32, (half, half), 1)
    row_cand, col_cand = row // slots, col // slots
    causal = (row_cand == col_cand) & (col <= row)
    masks = []
    for part in range(2):
        limit = jnp.zeros((half, half), jnp.int32)
        for j in range(per):
            limit = jnp.where(col_cand == j, lengths_ref[part * per + j] + j * slots, limit)
        masks.append(causal & (col < limit))

    def suffix_scores(h, r):
        return jnp.where(masks[r // half], scores(h, r, cand[0, r : r + half]), NEG_FILL)

    def suffix_rest(s, h, r):
        top = jnp.max(s, axis=1, keepdims=True)
        probs = jnp.exp2(s - top).astype(BF)
        acc[h, r : r + half] = jnp.dot(probs, with_ones(cand[1, r : r + half]), preferred_element_type=F32)
        row_max[h, r : r + half] = jnp.broadcast_to(top, (half, hd))

    ahead(pairs, suffix_scores, suffix_rest)

    def absorb(s, h, r, values, last):
        old = row_max[h, r : r + half]
        new = jnp.maximum(old, jnp.max(s, axis=1, keepdims=True))
        shrink = jnp.exp2(old - new)
        probs = jnp.exp2(s - new[:, :1]).astype(BF)
        added = jnp.dot(probs, with_ones(values), preferred_element_type=F32)
        result = acc[h, r : r + half] * jnp.concatenate([shrink, shrink], axis=1) + added
        if last:
            att[0, core, h, r : r + half] = (result[:, :hd] / result[:, hd:]).astype(BF)
        else:
            acc[h, r : r + half] = result
            row_max[h, r : r + half] = new

    def block(slot, chosen):
        ahead(
            chosen,
            lambda h, r: scores(h, r, kv[0, slot]),
            lambda s, h, r: absorb(s, h, r, kv[1, slot], False),
        )

    def both(slot):
        return kv[0, slot], kv[1, slot]

    every1 = range(CHUNKS1)
    local[0].wait()
    for c in every1:
        shared(1, 0, c)
    block(0, pairs)
    for c in every1:
        on_partner(1, c)
    for slot in (2, 3):
        for c in every1:
            on_plain(1, slot, c)
    for c in every1:
        shared(1, 1, c)
    block(1, pairs)
    for c in every1:
        on_far(1, c)
    for c in every1:
        shared(1, 2, c)
    block(2, pairs)
    for slot in (5, 6):
        for c in every1:
            on_plain(1, slot, c)
    for c in every1:
        shared(1, 3, c)
    block(3, pairs)
    for c in every1:
        on_plain(1, 7, c)
    for slot in (4, 5, 6, 7):
        for c in every1:
            shared(1, slot, c)

    def finish(h):
        units = [(h, r, j) for j in (0, 1) for r in (0, half)]

        def first(h, r, j):
            k = jnp.concatenate([kv[0, 4 + 2 * j], kv[0, 5 + 2 * j]], axis=0)
            return scores(h, r, k)

        def second(s, h, r, j):
            v = jnp.concatenate([kv[1, 4 + 2 * j], kv[1, 5 + 2 * j]], axis=0)
            absorb(s, h, r, v, j == 1)

        ahead(units, first, second)

    wide = total.shape[1]

    def project(slot, pair, first=False):
        dz = (0, 0, 1, 3, 2, 1, 3, 2)[slot]
        dx = (0, 1, 0, 0, 0, 1, 1, 1)[slot]
        group = lax.rem(z + dz, 4) * 2 + lax.rem(x_lo + dx, 2)
        base = group * (2 * heads * hd) + pair * 2 * hd
        pieces, sides = [], []
        for k in (0, 1):
            pieces += [att[slot, k, 2 * pair], att[slot, k, 2 * pair + 1]]
            start = pl.multiple_of(base + k * heads * hd, 2 * hd)
            sides.append(weights[pl.ds(start, 2 * hd), :])
        product = jnp.dot(
            jnp.concatenate(pieces, axis=1), jnp.concatenate(sides, axis=0), preferred_element_type=F32
        )
        total[...] = product if first else total[...] + product

    def launch(c):
        own_near(2, c)
        share(2, 0, c)
        own_far(2, c)

    finish(0)
    launch(0)
    finish(1)
    launch(1)
    finish(2)
    launch(2)
    on_partner(2, 0)
    finish(3)
    launch(3)

    def near_slots(c):
        on_plain(2, 2, c)
        on_plain(2, 3, c)

    def late_slots(c):
        on_plain(2, 5, c)
        on_plain(2, 6, c)

    def ready(slot, pair):
        shared(2, slot, 2 * pair)
        shared(2, slot, 2 * pair + 1)

    near_slots(0)
    on_partner(2, 1)
    on_far(2, 0)
    local[3].wait()
    ready(0, 0)
    project(0, 0, True)
    near_slots(1)
    late_slots(0)
    on_partner(2, 2)
    on_far(2, 1)
    on_plain(2, 7, 0)
    ready(1, 0)
    project(1, 0)
    near_slots(2)
    on_partner(2, 3)
    late_slots(1)
    ready(2, 0)
    project(2, 0)
    ready(3, 0)
    project(3, 0)
    on_far(2, 2)
    ready(4, 0)
    project(4, 0)
    on_plain(2, 7, 1)
    near_slots(3)
    ready(5, 0)
    project(5, 0)
    late_slots(2)
    ready(6, 0)
    project(6, 0)
    on_far(2, 3)
    ready(7, 0)
    project(7, 0)
    on_plain(2, 7, 2)
    for slot in (0, 1, 2, 3):
        ready(slot, 1)
        project(slot, 1)
    late_slots(3)
    ready(4, 1)
    project(4, 1)
    on_plain(2, 7, 3)
    for slot in (5, 6, 7):
        ready(slot, 1)
        project(slot, 1)
    out_ref[...] = total[...].astype(out_ref.dtype)

    cand_copy.wait_send()
    for copy in sent:
        copy.wait_send()


CHUNKS1 = 2


def body(queries, prefix_kv, cand_kv, lengths, out_weight):
    tokens, width = queries.shape
    hd = prefix_kv.shape[2]
    heads = width // hd
    positions = prefix_kv.shape[1]
    any_ = pl.BlockSpec(memory_space=pl.ANY)
    dma = pltpu.SemaphoreType.DMA
    return pl.pallas_call(
        attend_kernel,
        out_shape=jax.ShapeDtypeStruct((tokens, out_weight.shape[1]), BF),
        in_specs=[pl.BlockSpec(memory_space=pltpu.SMEM), any_, any_, any_, any_],
        out_specs=pl.BlockSpec(memory_space=pltpu.VMEM),
        scratch_shapes=[
            pltpu.VMEM((2, 8, positions, hd), BF),
            pltpu.VMEM((2, tokens, hd), BF),
            pltpu.VMEM((tokens, width), BF),
            pltpu.VMEM((heads, tokens, 2 * hd), BF),
            pltpu.VMEM(out_weight.shape, BF),
            pltpu.VMEM((heads, tokens, 2 * hd), F32),
            pltpu.VMEM((heads, tokens, hd), F32),
            pltpu.VMEM((8, 2, heads, tokens, hd), BF),
            pltpu.VMEM((tokens, out_weight.shape[1]), F32),
            dma((4,)),
            dma((2,)),
            dma((KINDS, CHUNKS1)),
            dma((8, CHUNKS1)),
            dma((8, CHUNKS1)),
            dma((KINDS, heads)),
            dma((8, heads)),
            dma((8, heads)),
        ],
        compiler_params=pltpu.CompilerParams(
            collective_id=0, has_side_effects=True, vmem_limit_bytes=60 * 1024 * 1024
        ),
        name="attend",
    )(lengths, queries, prefix_kv, cand_kv, out_weight)


def solution(mesh):
    placed = (
        P("ctx", "head"),
        P("head", "ctx", None),
        P("head", "ctx", None),
        P("ctx"),
        P(None, "head"),
    )
    return jax.shard_map(
        body, mesh=mesh, in_specs=placed, out_specs=P("ctx", "head"), check_vma=False
    )
```

```python
import functools
import math

import jax
import jax.numpy as jnp
from jax import lax
from jax.experimental import pallas as pl
from jax.experimental.pallas import tpu as pltpu
from jax.sharding import PartitionSpec as P

MESH = pl.DeviceIdType.MESH
BF = jnp.bfloat16
F32 = jnp.float32
NEG_FILL = -1e30
NT = (((1,), (1,)), ((), ()))

FORWARD, BACK, OVER = 0, 1, 2
KINDS = 15
CHUNKS1 = 2


def attend_kernel(
    lengths_ref, q_hbm, pre_hbm, cand_hbm, w_hbm, out_ref,
    kv, cand, q_raw, q_two, weights, acc, row_max, att, total,
    local_sem, cand_sem, s1, r1, b1, s2, r2, b2,
):
    ctx, head = lax.axis_index("ctx"), lax.axis_index("head")
    y, x_hi = ctx // 2, ctx % 2
    z, x_lo, core = head // 4, (head // 2) % 2, head % 2

    def ring1(d):
        return (lax.rem(y + d, 4) * 2 + x_hi, head)

    def ring2(d):
        return (ctx, lax.rem(z + d, 4) * 4 + x_lo * 2 + core)

    over1 = (y * 2 + 1 - x_hi, head)
    over2 = (ctx, z * 4 + (1 - x_lo) * 2 + core)
    sibling = (ctx, z * 4 + x_lo * 2 + 1 - core)
    near1 = {FORWARD: ring1(1), BACK: ring1(3), OVER: over1}
    near2 = {FORWARD: ring2(1), BACK: ring2(3), OVER: over2}

    barrier = pltpu.get_barrier_semaphore()
    others = [*near1.values(), *near2.values(), sibling]
    for other in others:
        pl.semaphore_signal(barrier, inc=1, device_id=other, device_id_type=MESH)

    local = [
        pltpu.make_async_copy(pre_hbm.at[0], kv.at[core, 0], local_sem.at[0]),
        pltpu.make_async_copy(cand_hbm.at[0], cand.at[core], local_sem.at[1]),
        pltpu.make_async_copy(q_hbm, q_raw, local_sem.at[2]),
        pltpu.make_async_copy(w_hbm, weights, local_sem.at[3]),
    ]
    for copy in local[:3]:
        copy.start()

    def remote(src, dst, send, recv, device):
        return pltpu.make_async_remote_copy(
            src_ref=src, dst_ref=dst, send_sem=send, recv_sem=recv, device_id=device, device_id_type=MESH
        )

    rows1 = kv.shape[2] // CHUNKS1

    def piece1(slot, c):
        return kv.at[core, slot, pl.ds(c * rows1, rows1)]

    def piece2(slot, c):
        return att.at[slot, core, c]

    sent = []

    def send(phase, src_slot, dst_slot, c, kind, device):
        piece, ss, rr = (piece1, s1, r1) if phase == 1 else (piece2, s2, r2)
        src = piece(src_slot, c)
        if phase == 1 and src_slot == 0:
            src = pre_hbm.at[0, pl.ds(c * rows1, rows1)]
        copy = remote(src, piece(dst_slot, c), ss.at[kind, c], rr.at[dst_slot, c], device)
        copy.start()
        sent.append(copy)

    def share(phase, slot, c):
        piece, ss, bb = (piece1, s1, b1) if phase == 1 else (piece2, s2, b2)
        src = piece(slot, c)
        if phase == 1 and slot == 0:
            src = pre_hbm.at[0, pl.ds(c * rows1, rows1)]
        copy = remote(src, piece(slot, c), ss.at[6 + slot, c], bb.at[slot, c], sibling)
        copy.start()
        sent.append(copy)

    def arrived(phase, slot, c):
        piece, rr = (piece1, r1) if phase == 1 else (piece2, r2)
        ref = piece(slot, c)
        remote(ref, ref, rr.at[slot, c], rr.at[slot, c], sibling).wait_recv()

    def shared(phase, slot, c):
        if phase == 1:
            ref, bb = kv.at[1 - core, slot, pl.ds(c * rows1, rows1)], b1
        else:
            ref, bb = att.at[slot, 1 - core, c], b2
        remote(ref, ref, bb.at[slot, c], bb.at[slot, c], sibling).wait_recv()

    def near(phase):
        return near1 if phase == 1 else near2

    def own(phase, c):
        n = near(phase)
        send(phase, 0, 1, c, 0, n[OVER])
        send(phase, 0, 3, c, 1, n[FORWARD])
        send(phase, 0, 2, c, 2, n[BACK])
        share(phase, 0, c)

    def on_near(phase, c):
        arrived(phase, 2 + c % 2, c)
        send(phase, 2 + c % 2, 4, c, 3, near(phase)[FORWARD if c % 2 else BACK])
        share(phase, 2 + c % 2, c)
        on_plain(phase, 3 - c % 2, c)

    def on_partner(phase, c):
        arrived(phase, 1, c)
        send(phase, 1, 6, c, 4, near(phase)[FORWARD])
        send(phase, 1, 5, c, 5, near(phase)[BACK])
        share(phase, 1, c)

    def on_far(phase, c):
        arrived(phase, 4, c)
        send(phase, 4, 7, c, 14, near(phase)[OVER])
        share(phase, 4, c)

    def on_late(phase, c):
        on_plain(phase, 5, c)
        on_plain(phase, 6, c)

    def on_last(phase, c):
        on_plain(phase, 7, c)

    def on_plain(phase, slot, c):
        arrived(phase, slot, c)
        share(phase, slot, c)

    heads = q_two.shape[0]
    hd = kv.shape[3]
    factor = hd ** (-0.5) * math.log2(math.e)
    local[2].wait()
    for h in range(heads):
        scaled = q_raw[:, h * hd : (h + 1) * hd].astype(F32) * factor
        high = scaled.astype(BF)
        q_two[h, :, :hd] = high
        q_two[h, :, hd:] = (scaled - high.astype(F32)).astype(BF)

    pl.semaphore_wait(barrier, len(others))

    cand_copy = remote(cand_hbm.at[0], cand.at[core], cand_sem.at[0], cand_sem.at[1], sibling)
    cand_copy.start()
    for c in range(CHUNKS1):
        own(1, c)
    local[3].start()

    tokens = q_two.shape[1]
    half = tokens // 2
    pairs = [(h, r) for h in range(heads) for r in (0, half)]

    def twice(k):
        return jnp.concatenate([k, k], axis=1)

    def with_ones(v):
        return jnp.concatenate([v, jnp.ones_like(v)], axis=1)

    def scores(h, r, keys):
        return lax.dot_general(q_two[h, r : r + half], twice(keys), NT, preferred_element_type=F32)

    def ahead(units, first, second):
        held = first(*units[0])
        for i, unit in enumerate(units):
            following = first(*units[i + 1]) if i + 1 < len(units) else None
            second(held, *unit)
            held = following

    local[1].wait()
    remote(cand.at[1 - core], cand.at[1 - core], cand_sem.at[0], cand_sem.at[1], sibling).wait_recv()
    slots = tokens // lengths_ref.shape[0]
    per = half // slots
    row = lax.broadcasted_iota(jnp.int32, (half, half), 0)
    col = lax.broadcasted_iota(jnp.int32, (half, half), 1)
    row_cand, col_cand = row // slots, col // slots
    causal = (row_cand == col_cand) & (col <= row)
    masks = []
    for part in range(2):
        limit = jnp.zeros((half, half), jnp.int32)
        for j in range(per):
            limit = jnp.where(col_cand == j, lengths_ref[part * per + j] + j * slots, limit)
        masks.append(causal & (col < limit))

    def suffix_scores(h, r):
        return jnp.where(masks[r // half], scores(h, r, cand[0, r : r + half]), NEG_FILL)

    def suffix_rest(s, h, r):
        top = jnp.max(s, axis=1, keepdims=True)
        probs = jnp.exp2(s - top).astype(BF)
        acc[h, r : r + half] = jnp.dot(probs, with_ones(cand[1, r : r + half]), preferred_element_type=F32)
        row_max[h, r : r + half] = jnp.broadcast_to(top, (half, hd))

    ahead(pairs, suffix_scores, suffix_rest)

    def absorb(s, h, r, values, last):
        old = row_max[h, r : r + half]
        new = jnp.maximum(old, jnp.max(s, axis=1, keepdims=True))
        shrink = jnp.exp2(old - new)
        probs = jnp.exp2(s - new[:, :1]).astype(BF)
        added = jnp.dot(probs, with_ones(values), preferred_element_type=F32)
        result = acc[h, r : r + half] * jnp.concatenate([shrink, shrink], axis=1) + added
        if last:
            att[0, core, h, r : r + half] = (result[:, :hd] / result[:, hd:]).astype(BF)
        else:
            acc[h, r : r + half] = result
            row_max[h, r : r + half] = new

    def keys_of(kind, pieces):
        parts = [kv[kind, slot, c * rows1 : (c + 1) * rows1] for slot, c in pieces]
        return jnp.concatenate(parts, axis=0) if len(parts) > 1 else parts[0]

    def attend(units):
        ahead(
            units,
            lambda h, r, pieces, last: scores(h, r, keys_of(0, pieces)),
            lambda s, h, r, pieces, last: absorb(s, h, r, keys_of(1, pieces), last),
        )

    def over(hs, pieces, last=False):
        return [(h, r, pieces, last) for h in hs for r in (0, half)]

    def whole(*chosen):
        return [(slot, c) for slot in chosen for c in every1]

    def await_shared(pieces):
        for slot, c in pieces:
            shared(1, slot, c)

    every1 = range(CHUNKS1)
    local[0].wait()
    await_shared(whole(0))
    attend(over((0, 1), whole(0)))
    on_near(1, 0)
    on_partner(1, 0)
    attend(over((2, 3), whole(0)))
    first, second = [(1, 0), (2, 0), (3, 0)], [(1, 1), (2, 1), (3, 1)]
    await_shared(first)
    attend(over((0, 1), first))
    on_near(1, 1)
    on_partner(1, 1)
    attend(over((2, 3), first))
    on_far(1, 0)
    await_shared(second)
    attend(over((0, 1), second))
    on_far(1, 1)
    on_late(1, 0)
    attend(over((2, 3), second))
    on_late(1, 1)
    await_shared(whole(4))
    attend(over(range(heads), whole(4)))
    on_last(1, 0)
    on_last(1, 1)
    await_shared(whole(5, 6))
    attend(over((0,), whole(5, 6)))
    await_shared(whole(7))

    def finish(h):
        attend((over((h,), whole(5, 6)) if h else []) + over((h,), whole(7), True))

    wide = total.shape[1]

    def project(slot, pair, first=False):
        dz = (0, 0, 1, 3, 2, 1, 3, 2)[slot]
        dx = (0, 1, 0, 0, 0, 1, 1, 1)[slot]
        group = lax.rem(z + dz, 4) * 2 + lax.rem(x_lo + dx, 2)
        base = group * (2 * heads * hd) + pair * 2 * hd
        pieces, sides = [], []
        for k in (0, 1):
            pieces += [att[slot, k, 2 * pair], att[slot, k, 2 * pair + 1]]
            start = pl.multiple_of(base + k * heads * hd, 2 * hd)
            sides.append(weights[pl.ds(start, 2 * hd), :])
        product = jnp.dot(
            jnp.concatenate(pieces, axis=1), jnp.concatenate(sides, axis=0), preferred_element_type=F32
        )
        total[...] = product if first else total[...] + product

    def ready(slot, pair):
        shared(2, slot, 2 * pair)
        shared(2, slot, 2 * pair + 1)

    def take(slot, pair):
        ready(slot, pair)
        project(slot, pair, slot == 0 and pair == 0)

    finish(0)
    own(2, 0)
    finish(1)
    own(2, 1)
    finish(2)
    own(2, 2)
    on_near(2, 0)
    finish(3)
    own(2, 3)
    on_near(2, 1)
    on_partner(2, 0)
    local[3].wait()
    take(0, 0)
    on_near(2, 2)
    on_partner(2, 1)
    on_far(2, 0)
    take(1, 0)
    take(2, 0)
    take(3, 0)
    on_near(2, 3)
    on_partner(2, 2)
    on_far(2, 1)
    take(0, 1)
    on_late(2, 0)
    on_partner(2, 3)
    on_last(2, 0)
    take(1, 1)
    take(2, 1)
    take(3, 1)
    on_far(2, 2)
    take(4, 0)
    on_late(2, 1)
    take(5, 0)
    take(6, 0)
    on_last(2, 1)
    take(7, 0)
    on_far(2, 3)
    take(4, 1)
    on_late(2, 2)
    on_last(2, 2)
    on_late(2, 3)
    take(5, 1)
    take(6, 1)
    on_last(2, 3)
    take(7, 1)
    out_ref[...] = total[...].astype(out_ref.dtype)

    cand_copy.wait_send()
    for copy in sent:
        copy.wait_send()


def body(queries, prefix_kv, cand_kv, lengths, out_weight):
    tokens, width = queries.shape
    hd = prefix_kv.shape[2]
    heads = width // hd
    positions = prefix_kv.shape[1]
    any_ = pl.BlockSpec(memory_space=pl.ANY)
    args = [
        pltpu.with_memory_space_constraint(a, pltpu.HBM)
        for a in (lengths, queries, prefix_kv, cand_kv, out_weight)
    ]
    dma = pltpu.SemaphoreType.DMA
    return pl.pallas_call(
        attend_kernel,
        out_shape=jax.ShapeDtypeStruct((tokens, out_weight.shape[1]), BF),
        in_specs=[pl.BlockSpec(memory_space=pltpu.SMEM), any_, any_, any_, any_],
        out_specs=pl.BlockSpec(memory_space=pltpu.VMEM),
        scratch_shapes=[
            pltpu.VMEM((2, 8, positions, hd), BF),
            pltpu.VMEM((2, tokens, hd), BF),
            pltpu.VMEM((tokens, width), BF),
            pltpu.VMEM((heads, tokens, 2 * hd), BF),
            pltpu.VMEM(out_weight.shape, BF),
            pltpu.VMEM((heads, tokens, 2 * hd), F32),
            pltpu.VMEM((heads, tokens, hd), F32),
            pltpu.VMEM((8, 2, heads, tokens, hd), BF),
            pltpu.VMEM((tokens, out_weight.shape[1]), F32),
            dma((4,)),
            dma((2,)),
            dma((KINDS, CHUNKS1)),
            dma((8, CHUNKS1)),
            dma((8, CHUNKS1)),
            dma((KINDS, heads)),
            dma((8, heads)),
            dma((8, heads)),
        ],
        compiler_params=pltpu.CompilerParams(
            collective_id=0, has_side_effects=True, vmem_limit_bytes=48 * 1024 * 1024
        ),
        name="attend",
    )(*args)


def solution(mesh):
    placed = (
        P("ctx", "head"),
        P("head", "ctx", None),
        P("head", "ctx", None),
        P("ctx"),
        P(None, "head"),
    )
    return jax.shard_map(
        body, mesh=mesh, in_specs=placed, out_specs=P("ctx", "head"), check_vma=False
    )
```

```python
import functools
import math

import jax
import jax.numpy as jnp
from jax import lax
from jax.experimental import pallas as pl
from jax.experimental.pallas import tpu as pltpu
from jax.sharding import PartitionSpec as P

MESH = pl.DeviceIdType.MESH
BF = jnp.bfloat16
F32 = jnp.float32
NEG_FILL = -1e30
NT = (((1,), (1,)), ((), ()))

FORWARD, BACK, OVER = 0, 1, 2
KINDS = 17
CHUNKS1 = 2
ARRIVE, ATTEND, LAUNCH, PROJECT = range(4)
SPLIT = 3
SCHEDULE = (
    (ATTEND, (3, ((0, 0), (0, 1))), (1, ((0, 1),)), (2, ((0, 0), (0, 1))), (0, ((0, 1),))),
    (ARRIVE, 1, 2, 0),
    (ARRIVE, 1, 3, 0),
    (ATTEND, (0, ((0, 0),))),
    (ARRIVE, 1, 2, 1),
    (ARRIVE, 1, 3, 1),
    (ARRIVE, 1, 1, 0),
    (ARRIVE, 1, 1, 1),
    (ATTEND, (2, ((2, 0), (3, 0))), (3, ((2, 0),)), (1, ((2, 0),)), (0, ((2, 0),))),
    (ARRIVE, 1, 4, 0),
    (ATTEND, (3, ((1, 0), (1, 1), (3, 1))), (1, ((0, 0), (1, 0))), (2, ((1, 0), (1, 1), (2, 1)))),
    (ARRIVE, 1, 4, 1),
    (ARRIVE, 1, 5, 0),
    (ATTEND, (3, ((2, 1), (4, 0))), (1, ((1, 1), (3, 0), (3, 1), (4, 0))), (2, ((3, 1), (4, 0))), (0, ((3, 1),))),
    (ARRIVE, 1, 6, 0),
    (ARRIVE, 1, 5, 1),
    (ATTEND, (2, ((4, 1), (5, 0))), (3, ((3, 0), (4, 1), (5, 0)))),
    (ARRIVE, 1, 6, 1),
    (ARRIVE, 1, 7, 0),
    (ARRIVE, 1, 7, 1),
    (ATTEND, (3, ((5, 1), (6, 0))), (2, ((5, 1), (6, 0))), (1, ((2, 1),))),
    (ATTEND, (3, ((6, 1), (7, 0), (7, 1)))),
    (LAUNCH, 3),
    (ATTEND, (2, ((6, 1), (7, 0), (7, 1)))),
    (LAUNCH, 2),
    (ATTEND, (1, ((4, 1), (5, 0), (5, 1), (6, 0), (6, 1), (7, 0), (7, 1)))),
    (LAUNCH, 1),
    (ATTEND, (0, ((1, 0), (1, 1), (2, 1), (3, 0), (4, 0), (4, 1), (5, 0), (5, 1), (6, 0), (6, 1), (7, 0), (7, 1)))),
    (ARRIVE, 2, 3, 3),
    (LAUNCH, 0),
    (ARRIVE, 2, 2, 2),
    (ARRIVE, 2, 3, 2),
    (ARRIVE, 2, 2, 3),
    (ARRIVE, 2, 3, 1),
    (ARRIVE, 2, 1, 3),
    (ARRIVE, 2, 2, 0),
    (ARRIVE, 2, 4, 3),
    (ARRIVE, 2, 1, 2),
    (ARRIVE, 2, 4, 2),
    (ARRIVE, 2, 2, 1),
    (ARRIVE, 2, 3, 0),
    (ARRIVE, 2, 1, 0),
    (PROJECT, 0, 1),
    (ARRIVE, 2, 4, 1),
    (ARRIVE, 2, 4, 0),
    (ARRIVE, 2, 1, 1),
    (ARRIVE, 2, 7, 2),
    (ARRIVE, 2, 5, 2),
    (PROJECT, 3, 1),
    (PROJECT, 4, 1),
    (ARRIVE, 2, 7, 3),
    (PROJECT, 3, 0),
    (PROJECT, 2, 1),
    (ARRIVE, 2, 5, 3),
    (PROJECT, 1, 1),
    (ARRIVE, 2, 6, 3),
    (PROJECT, 2, 0),
    (PROJECT, 1, 0),
    (ARRIVE, 2, 7, 1),
    (PROJECT, 4, 0),
    (ARRIVE, 2, 6, 2),
    (PROJECT, 0, 0),
    (ARRIVE, 2, 7, 0),
    (ARRIVE, 2, 6, 0),
    (PROJECT, 5, 1),
    (ARRIVE, 2, 6, 1),
    (ARRIVE, 2, 5, 0),
    (ARRIVE, 2, 5, 1),
    (PROJECT, 6, 1),
    (PROJECT, 7, 1),
    (PROJECT, 7, 0),
    (PROJECT, 6, 0),
    (PROJECT, 5, 0),
)


def attend_kernel(
    lengths_hbm, q_hbm, pre_hbm, cand_hbm, w_hbm, out_ref,
    kv, cand, q_raw, q_two, weights, acc, row_max, att, total,
    lengths_ref, local_sem, cand_sem, s1, r1, b1, s2, r2, b2,
):
    ctx, head = lax.axis_index("ctx"), lax.axis_index("head")
    y, x_hi = ctx // 2, ctx % 2
    z, x_lo, core = head // 4, (head // 2) % 2, head % 2

    def ring1(d):
        return (lax.rem(y + d, 4) * 2 + x_hi, head)

    def ring2(d):
        return (ctx, lax.rem(z + d, 4) * 4 + x_lo * 2 + core)

    over1 = (y * 2 + 1 - x_hi, head)
    over2 = (ctx, z * 4 + (1 - x_lo) * 2 + core)
    sibling = (ctx, z * 4 + x_lo * 2 + 1 - core)
    near1 = {FORWARD: ring1(1), BACK: ring1(3), OVER: over1}
    near2 = {FORWARD: ring2(1), BACK: ring2(3), OVER: over2}

    barrier = pltpu.get_barrier_semaphore()
    others = [*near1.values(), *near2.values(), sibling]
    for other in others:
        pl.semaphore_signal(barrier, inc=1, device_id=other, device_id_type=MESH)

    local = [
        pltpu.make_async_copy(pre_hbm.at[0], kv.at[core, 0], local_sem.at[0]),
        pltpu.make_async_copy(cand_hbm.at[0], cand.at[core], local_sem.at[1]),
        pltpu.make_async_copy(q_hbm, q_raw, local_sem.at[2]),
        pltpu.make_async_copy(w_hbm, weights, local_sem.at[3]),
        pltpu.make_async_copy(lengths_hbm, lengths_ref, local_sem.at[4]),
    ]
    for copy in local[:3] + local[4:]:
        copy.start()

    def remote(src, dst, send, recv, device):
        return pltpu.make_async_remote_copy(
            src_ref=src, dst_ref=dst, send_sem=send, recv_sem=recv, device_id=device, device_id_type=MESH
        )

    rows1 = kv.shape[2] // CHUNKS1

    def piece1(slot, c):
        return kv.at[core, slot, pl.ds(c * rows1, rows1)]

    def piece2(slot, c):
        return att.at[slot, core, c]

    sent = []

    def send(phase, src_slot, dst_slot, c, kind, device):
        piece, ss, rr = (piece1, s1, r1) if phase == 1 else (piece2, s2, r2)
        src = piece(src_slot, c)
        if phase == 1 and src_slot == 0:
            src = pre_hbm.at[0, pl.ds(c * rows1, rows1)]
        copy = remote(src, piece(dst_slot, c), ss.at[kind, c], rr.at[dst_slot, c], device)
        copy.start()
        sent.append(copy)

    def send_half(src_slot, dst_slot, part, kind, device):
        rows = att.shape[3] // 2
        src = piece2(src_slot, SPLIT).at[pl.ds(part * rows, rows)]
        dst = piece2(dst_slot, SPLIT).at[pl.ds(part * rows, rows)]
        recv = r2.at[dst_slot, SPLIT] if part == 0 else r2.at[dst_slot + 3, SPLIT]
        copy = remote(src, dst, s2.at[kind, SPLIT], recv, device)
        copy.start()
        sent.append(copy)

    def share(phase, slot, c):
        piece, ss, bb = (piece1, s1, b1) if phase == 1 else (piece2, s2, b2)
        src = piece(slot, c)
        if phase == 1 and slot == 0:
            src = pre_hbm.at[0, pl.ds(c * rows1, rows1)]
        copy = remote(src, piece(slot, c), ss.at[6 + slot, c], bb.at[slot, c], sibling)
        copy.start()
        sent.append(copy)

    def arrived(phase, slot, c):
        piece, rr = (piece1, r1) if phase == 1 else (piece2, r2)
        ref = piece(slot, c)
        if phase == 2 and c == SPLIT and slot in (5, 6):
            for part in (0, 1):
                rows = att.shape[3] // 2
                half_ref = ref.at[pl.ds(part * rows, rows)]
                sem = rr.at[slot + 3 * part, c]
                remote(half_ref, half_ref, sem, sem, sibling).wait_recv()
        else:
            remote(ref, ref, rr.at[slot, c], rr.at[slot, c], sibling).wait_recv()

    def shared(phase, slot, c):
        if phase == 1:
            ref, bb = kv.at[1 - core, slot, pl.ds(c * rows1, rows1)], b1
        else:
            ref, bb = att.at[slot, 1 - core, c], b2
        remote(ref, ref, bb.at[slot, c], bb.at[slot, c], sibling).wait_recv()

    def near(phase):
        return near1 if phase == 1 else near2

    def own(phase, c):
        n = near(phase)
        send(phase, 0, 1, c, 0, n[OVER])
        send(phase, 0, 3, c, 1, n[FORWARD])
        send(phase, 0, 2, c, 2, n[BACK])
        share(phase, 0, c)

    def on_arrival(phase, slot, c):
        n = near(phase)
        arrived(phase, slot, c)
        divided = phase == 2 and c == SPLIT
        if slot == 1 and divided:
            send_half(1, 6, 0, 4, n[FORWARD])
            send_half(1, 5, 0, 5, n[BACK])
        elif slot == 1:
            send(phase, 1, 6, c, 4, n[FORWARD])
            send(phase, 1, 5, c, 5, n[BACK])
        if slot in (2, 3) and divided:
            send_half(slot, slot + 3, 1, 13 + slot, n[OVER])
        if slot == 2 and c % 2 == 0:
            send(phase, 2, 4, c, 3, n[BACK])
        if slot == 3 and c % 2 == 1:
            send(phase, 3, 4, c, 3, n[FORWARD])
        if slot == 4:
            send(phase, 4, 7, c, 14, n[OVER])
        share(phase, slot, c)

    heads = q_two.shape[0]
    hd = kv.shape[3]
    factor = hd ** (-0.5) * math.log2(math.e)
    local[2].wait()
    for h in range(heads):
        scaled = q_raw[:, h * hd : (h + 1) * hd].astype(F32) * factor
        high = scaled.astype(BF)
        q_two[h, :, :hd] = high
        q_two[h, :, hd:] = (scaled - high.astype(F32)).astype(BF)

    pl.semaphore_wait(barrier, len(others))

    cand_copy = remote(cand_hbm.at[0], cand.at[core], cand_sem.at[0], cand_sem.at[1], sibling)
    cand_copy.start()
    for c in range(CHUNKS1):
        own(1, c)
    local[3].start()

    tokens = q_two.shape[1]
    half = tokens // 2
    pairs = [(h, r) for h in range(heads) for r in (0, half)]

    def twice(k):
        return jnp.concatenate([k, k], axis=1)

    def with_ones(v):
        return jnp.concatenate([v, jnp.ones_like(v)], axis=1)

    def scores(h, r, keys):
        return lax.dot_general(q_two[h, r : r + half], twice(keys), NT, preferred_element_type=F32)

    def ahead(units, first, second):
        held = first(*units[0])
        for i, unit in enumerate(units):
            following = first(*units[i + 1]) if i + 1 < len(units) else None
            second(held, *unit)
            held = following

    local[1].wait()
    local[4].wait()
    remote(cand.at[1 - core], cand.at[1 - core], cand_sem.at[0], cand_sem.at[1], sibling).wait_recv()
    slots = tokens // lengths_ref.shape[0]
    per = half // slots
    row = lax.broadcasted_iota(jnp.int32, (half, half), 0)
    col = lax.broadcasted_iota(jnp.int32, (half, half), 1)
    row_cand, col_cand = row // slots, col // slots
    causal = (row_cand == col_cand) & (col <= row)
    masks = []
    for part in range(2):
        limit = jnp.zeros((half, half), jnp.int32)
        for j in range(per):
            limit = jnp.where(col_cand == j, lengths_ref[part * per + j] + j * slots, limit)
        masks.append(causal & (col < limit))

    def suffix_scores(h, r):
        return jnp.where(masks[r // half], scores(h, r, cand[0, r : r + half]), NEG_FILL)

    def suffix_rest(s, h, r):
        top = jnp.max(s, axis=1, keepdims=True)
        probs = jnp.exp2(s - top).astype(BF)
        acc[h, r : r + half] = jnp.dot(probs, with_ones(cand[1, r : r + half]), preferred_element_type=F32)
        row_max[h, r : r + half] = jnp.broadcast_to(top, (half, hd))

    ahead(pairs, suffix_scores, suffix_rest)

    def absorb(s, h, r, values, last):
        old = row_max[h, r : r + half]
        new = jnp.maximum(old, jnp.max(s, axis=1, keepdims=True))
        shrink = jnp.exp2(old - new)
        probs = jnp.exp2(s - new[:, :1]).astype(BF)
        added = jnp.dot(probs, with_ones(values), preferred_element_type=F32)
        result = acc[h, r : r + half] * jnp.concatenate([shrink, shrink], axis=1) + added
        if last:
            att[0, core, h, r : r + half] = (result[:, :hd] / result[:, hd:]).astype(BF)
        else:
            acc[h, r : r + half] = result
            row_max[h, r : r + half] = new

    def keys_of(kind, pieces):
        parts = [kv[kind, slot, c * rows1 : (c + 1) * rows1] for slot, c in pieces]
        return jnp.concatenate(parts, axis=0) if len(parts) > 1 else parts[0]

    def attend(units):
        ahead(
            units,
            lambda h, r, pieces, last: scores(h, r, keys_of(0, pieces)),
            lambda s, h, r, pieces, last: absorb(s, h, r, keys_of(1, pieces), last),
        )

    wide = total.shape[1]

    def project(slot, pair, first=False):
        dz = (0, 0, 1, 3, 2, 1, 3, 2)[slot]
        dx = (0, 1, 0, 0, 0, 1, 1, 1)[slot]
        group = lax.rem(z + dz, 4) * 2 + lax.rem(x_lo + dx, 2)
        base = group * (2 * heads * hd) + pair * 2 * hd
        pieces, sides = [], []
        for k in (0, 1):
            pieces += [att[slot, k, 2 * pair], att[slot, k, 2 * pair + 1]]
            start = pl.multiple_of(base + k * heads * hd, 2 * hd)
            sides.append(weights[pl.ds(start, 2 * hd), :])
        product = jnp.dot(
            jnp.concatenate(pieces, axis=1), jnp.concatenate(sides, axis=0), preferred_element_type=F32
        )
        total[...] = product if first else total[...] + product

    local[0].wait()
    here, left, projected = set(), [8 * CHUNKS1] * heads, 0
    for step in SCHEDULE:
        if step[0] == ARRIVE:
            on_arrival(*step[1:])
        elif step[0] == ATTEND:
            units = []
            for h, pieces in step[1:]:
                for piece in pieces:
                    if piece not in here:
                        here.add(piece)
                        shared(1, *piece)
                left[h] -= len(pieces)
                units += [(h, r, pieces, left[h] == 0) for r in (0, half)]
            attend(units)
        elif step[0] == LAUNCH:
            own(2, step[1])
        else:
            slot, pair = step[1:]
            shared(2, slot, 2 * pair)
            shared(2, slot, 2 * pair + 1)
            if projected == 0:
                local[3].wait()
            project(slot, pair, projected == 0)
            projected += 1
    out_ref[...] = total[...].astype(out_ref.dtype)

    cand_copy.wait_send()
    for copy in sent:
        copy.wait_send()


def body(queries, prefix_kv, cand_kv, lengths, out_weight):
    tokens, width = queries.shape
    hd = prefix_kv.shape[2]
    heads = width // hd
    positions = prefix_kv.shape[1]
    any_ = pl.BlockSpec(memory_space=pl.ANY)
    args = [
        pltpu.with_memory_space_constraint(a, pltpu.HBM)
        for a in (lengths, queries, prefix_kv, cand_kv, out_weight)
    ]
    dma = pltpu.SemaphoreType.DMA
    return pl.pallas_call(
        attend_kernel,
        out_shape=jax.ShapeDtypeStruct((tokens, out_weight.shape[1]), BF),
        in_specs=[any_] * 5,
        out_specs=pl.BlockSpec(memory_space=pltpu.VMEM),
        scratch_shapes=[
            pltpu.VMEM((2, 8, positions, hd), BF),
            pltpu.VMEM((2, tokens, hd), BF),
            pltpu.VMEM((tokens, width), BF),
            pltpu.VMEM((heads, tokens, 2 * hd), BF),
            pltpu.VMEM(out_weight.shape, BF),
            pltpu.VMEM((heads, tokens, 2 * hd), F32),
            pltpu.VMEM((heads, tokens, hd), F32),
            pltpu.VMEM((8, 2, heads, tokens, hd), BF),
            pltpu.VMEM((tokens, out_weight.shape[1]), F32),
            pltpu.SMEM(lengths.shape, jnp.int32),
            dma((5,)),
            dma((2,)),
            dma((KINDS, CHUNKS1)),
            dma((8, CHUNKS1)),
            dma((8, CHUNKS1)),
            dma((KINDS, heads)),
            dma((10, heads)),
            dma((8, heads)),
        ],
        compiler_params=pltpu.CompilerParams(
            collective_id=0, has_side_effects=True, vmem_limit_bytes=48 * 1024 * 1024
        ),
        name="attend",
    )(*args)


def solution(mesh):
    placed = (
        P("ctx", "head"),
        P("head", "ctx", None),
        P("head", "ctx", None),
        P("ctx"),
        P(None, "head"),
    )
    return jax.shard_map(
        body, mesh=mesh, in_specs=placed, out_specs=P("ctx", "head"), check_vma=False
    )
```

```python
import functools
import math

import jax
import jax.numpy as jnp
from jax import lax
from jax.experimental import pallas as pl
from jax.experimental.pallas import tpu as pltpu
from jax.sharding import PartitionSpec as P

MESH = pl.DeviceIdType.MESH
BF = jnp.bfloat16
F32 = jnp.float32
NEG_FILL = -1e30
NT = (((1,), (1,)), ((), ()))

FORWARD, BACK, OVER = 0, 1, 2
KINDS = 15
CHUNKS1 = 2
ARRIVE, ATTEND, LAUNCH, PROJECT = range(4)
TURNED = 2
SCHEDULE = (
    (ARRIVE, 1, 2, 0),
    (ATTEND, (0, ((0, 1),)), (1, ((0, 0), (0, 1))), (2, ((0, 0),))),
    (ARRIVE, 1, 3, 0),
    (ARRIVE, 1, 2, 1),
    (ARRIVE, 1, 3, 1),
    (ARRIVE, 1, 1, 0),
    (ARRIVE, 1, 1, 1),
    (ATTEND, (3, ((0, 1), (3, 0))), (2, ((2, 0), (3, 0))), (0, ((0, 0),))),
    (ARRIVE, 1, 4, 0),
    (ATTEND, (0, ((1, 0), (1, 1), (2, 0), (2, 1))), (3, ((0, 0), (2, 0), (2, 1))), (2, ((2, 1),))),
    (ARRIVE, 1, 4, 1),
    (ARRIVE, 1, 5, 0),
    (ATTEND, (3, ((1, 0), (1, 1), (4, 0))), (0, ((3, 0), (3, 1), (4, 0))), (2, ((4, 0),)), (1, ((1, 0),))),
    (ARRIVE, 1, 6, 0),
    (ARRIVE, 1, 5, 1),
    (ATTEND, (3, ((3, 1), (5, 0))), (2, ((0, 1), (3, 1), (5, 0))), (0, ((5, 0),))),
    (ARRIVE, 1, 6, 1),
    (ARRIVE, 1, 7, 0),
    (ARRIVE, 1, 7, 1),
    (ATTEND, (3, ((4, 1), (5, 1), (6, 0))), (0, ((4, 1), (6, 0))), (2, ((1, 1),))),
    (ATTEND, (3, ((6, 1), (7, 0), (7, 1)))),
    (LAUNCH, 3),
    (ATTEND, (0, ((5, 1), (6, 1), (7, 0), (7, 1)))),
    (LAUNCH, 0),
    (ATTEND, (2, ((1, 0), (4, 1), (5, 1), (6, 0), (6, 1), (7, 0), (7, 1)))),
    (LAUNCH, 2),
    (ATTEND, (1, ((1, 1), (2, 0), (2, 1), (3, 0), (3, 1), (4, 0), (4, 1), (5, 0), (5, 1), (6, 0), (6, 1), (7, 0), (7, 1)))),
    (LAUNCH, 1),
    (ARRIVE, 2, 2, 0),
    (ARRIVE, 2, 3, 2),
    (ARRIVE, 2, 2, 2),
    (ARRIVE, 2, 3, 3),
    (ARRIVE, 2, 3, 1),
    (PROJECT, 3, 1),
    (ARRIVE, 2, 1, 3),
    (ARRIVE, 2, 1, 2),
    (ARRIVE, 2, 3, 0),
    (ARRIVE, 2, 4, 3),
    (ARRIVE, 2, 1, 0),
    (ARRIVE, 2, 1, 1),
    (PROJECT, 0, 1),
    (ARRIVE, 2, 4, 2),
    (ARRIVE, 2, 4, 0),
    (ARRIVE, 2, 4, 1),
    (ARRIVE, 2, 7, 3),
    (ARRIVE, 2, 2, 1),
    (ARRIVE, 2, 5, 2),
    (ARRIVE, 2, 6, 3),
    (ARRIVE, 2, 2, 3),
    (PROJECT, 1, 0),
    (PROJECT, 0, 0),
    (PROJECT, 4, 0),
    (PROJECT, 4, 1),
    (ARRIVE, 2, 6, 2),
    (PROJECT, 2, 0),
    (ARRIVE, 2, 6, 0),
    (PROJECT, 3, 0),
    (ARRIVE, 2, 5, 0),
    (ARRIVE, 2, 5, 3),
    (PROJECT, 6, 1),
    (PROJECT, 2, 1),
    (ARRIVE, 2, 6, 1),
    (PROJECT, 1, 1),
    (ARRIVE, 2, 5, 1),
    (ARRIVE, 2, 7, 0),
    (ARRIVE, 2, 7, 1),
    (PROJECT, 5, 1),
    (ARRIVE, 2, 7, 2),
    (PROJECT, 6, 0),
    (PROJECT, 5, 0),
    (PROJECT, 7, 0),
    (PROJECT, 7, 1),
)


def attend_kernel(
    lengths_hbm, q_hbm, pre_hbm, cand_hbm, w_hbm, out_ref,
    kv, cand, q_raw, q_two, weights, acc, row_max, att, total,
    lengths_ref, local_sem, cand_sem, s1, r1, b1, s2, r2, b2,
):
    ctx, head = lax.axis_index("ctx"), lax.axis_index("head")
    y, x_hi = ctx // 2, ctx % 2
    z, x_lo, core = head // 4, (head // 2) % 2, head % 2

    def ring1(d):
        return (lax.rem(y + d, 4) * 2 + x_hi, head)

    def ring2(d):
        return (ctx, lax.rem(z + d, 4) * 4 + x_lo * 2 + core)

    over1 = (y * 2 + 1 - x_hi, head)
    over2 = (ctx, z * 4 + (1 - x_lo) * 2 + core)
    sibling = (ctx, z * 4 + x_lo * 2 + 1 - core)
    near1 = {FORWARD: ring1(1), BACK: ring1(3), OVER: over1}
    near2 = {FORWARD: ring2(1), BACK: ring2(3), OVER: over2}

    barrier = pltpu.get_barrier_semaphore()
    others = [*near1.values(), *near2.values(), sibling]
    for other in others:
        pl.semaphore_signal(barrier, inc=1, device_id=other, device_id_type=MESH)

    local = [
        pltpu.make_async_copy(pre_hbm.at[0], kv.at[core, 0], local_sem.at[0]),
        pltpu.make_async_copy(cand_hbm.at[0], cand.at[core], local_sem.at[1]),
        pltpu.make_async_copy(q_hbm, q_raw, local_sem.at[2]),
        pltpu.make_async_copy(w_hbm, weights, local_sem.at[3]),
        pltpu.make_async_copy(lengths_hbm, lengths_ref, local_sem.at[4]),
    ]
    for copy in local[:3] + local[4:]:
        copy.start()

    def remote(src, dst, send, recv, device):
        return pltpu.make_async_remote_copy(
            src_ref=src, dst_ref=dst, send_sem=send, recv_sem=recv, device_id=device, device_id_type=MESH
        )

    rows1 = kv.shape[2] // CHUNKS1

    def piece1(slot, c):
        return kv.at[core, slot, pl.ds(c * rows1, rows1)]

    def piece2(slot, c):
        return att.at[slot, core, c]

    sent = []

    def send(phase, src_slot, dst_slot, c, kind, device):
        piece, ss, rr = (piece1, s1, r1) if phase == 1 else (piece2, s2, r2)
        src = piece(src_slot, c)
        if phase == 1 and src_slot == 0:
            src = pre_hbm.at[0, pl.ds(c * rows1, rows1)]
        copy = remote(src, piece(dst_slot, c), ss.at[kind, c], rr.at[dst_slot, c], device)
        copy.start()
        sent.append(copy)

    def share(phase, slot, c):
        piece, ss, bb = (piece1, s1, b1) if phase == 1 else (piece2, s2, b2)
        src = piece(slot, c)
        if phase == 1 and slot == 0:
            src = pre_hbm.at[0, pl.ds(c * rows1, rows1)]
        copy = remote(src, piece(slot, c), ss.at[6 + slot, c], bb.at[slot, c], sibling)
        copy.start()
        sent.append(copy)

    def arrived(phase, slot, c):
        piece, rr = (piece1, r1) if phase == 1 else (piece2, r2)
        ref = piece(slot, c)
        remote(ref, ref, rr.at[slot, c], rr.at[slot, c], sibling).wait_recv()

    def shared(phase, slot, c):
        if phase == 1:
            ref, bb = kv.at[1 - core, slot, pl.ds(c * rows1, rows1)], b1
        else:
            ref, bb = att.at[slot, 1 - core, c], b2
        remote(ref, ref, bb.at[slot, c], bb.at[slot, c], sibling).wait_recv()

    def near(phase):
        return near1 if phase == 1 else near2

    def own(phase, c):
        n = near(phase)
        send(phase, 0, 1, c, 0, n[OVER])
        send(phase, 0, 3, c, 1, n[FORWARD])
        send(phase, 0, 2, c, 2, n[BACK])
        share(phase, 0, c)

    def on_arrival(phase, slot, c):
        n = near(phase)
        arrived(phase, slot, c)
        turned = phase == 2 and c == TURNED
        if slot == 1 and not turned:
            send(phase, 1, 6, c, 4, n[FORWARD])
            send(phase, 1, 5, c, 5, n[BACK])
        if slot in (2, 3) and turned:
            send(phase, slot, slot + 3, c, 2 + slot, n[OVER])
        if slot == 5 + c % 2 and turned:
            send(phase, slot, 7, c, 14, n[FORWARD if c % 2 else BACK])
        if slot == 2 and c % 2 == 0:
            send(phase, 2, 4, c, 3, n[BACK])
        if slot == 3 and c % 2 == 1:
            send(phase, 3, 4, c, 3, n[FORWARD])
        if slot == 4 and not turned:
            send(phase, 4, 7, c, 14, n[OVER])
        share(phase, slot, c)

    heads = q_two.shape[0]
    hd = kv.shape[3]
    factor = hd ** (-0.5) * math.log2(math.e)
    local[2].wait()
    for h in range(heads):
        scaled = q_raw[:, h * hd : (h + 1) * hd].astype(F32) * factor
        high = scaled.astype(BF)
        q_two[h, :, :hd] = high
        q_two[h, :, hd:] = (scaled - high.astype(F32)).astype(BF)

    pl.semaphore_wait(barrier, len(others))

    cand_copy = remote(cand_hbm.at[0], cand.at[core], cand_sem.at[0], cand_sem.at[1], sibling)
    cand_copy.start()
    for c in range(CHUNKS1):
        own(1, c)
    local[3].start()

    tokens = q_two.shape[1]
    half = tokens // 2
    pairs = [(h, r) for h in range(heads) for r in (0, half)]

    def twice(k):
        return jnp.concatenate([k, k], axis=1)

    def with_ones(v):
        return jnp.concatenate([v, jnp.ones_like(v)], axis=1)

    def scores(h, r, keys):
        return lax.dot_general(q_two[h, r : r + half], twice(keys), NT, preferred_element_type=F32)

    def ahead(units, first, second):
        held = first(*units[0])
        for i, unit in enumerate(units):
            following = first(*units[i + 1]) if i + 1 < len(units) else None
            second(held, *unit)
            held = following

    local[1].wait()
    local[4].wait()
    remote(cand.at[1 - core], cand.at[1 - core], cand_sem.at[0], cand_sem.at[1], sibling).wait_recv()
    slots = tokens // lengths_ref.shape[0]
    per = half // slots
    row = lax.broadcasted_iota(jnp.int32, (half, half), 0)
    col = lax.broadcasted_iota(jnp.int32, (half, half), 1)
    row_cand, col_cand = row // slots, col // slots
    causal = (row_cand == col_cand) & (col <= row)
    masks = []
    for part in range(2):
        limit = jnp.zeros((half, half), jnp.int32)
        for j in range(per):
            limit = jnp.where(col_cand == j, lengths_ref[part * per + j] + j * slots, limit)
        masks.append(causal & (col < limit))

    def suffix_scores(h, r):
        return jnp.where(masks[r // half], scores(h, r, cand[0, r : r + half]), NEG_FILL)

    def suffix_rest(s, h, r):
        top = jnp.max(s, axis=1, keepdims=True)
        probs = jnp.exp2(s - top).astype(BF)
        acc[h, r : r + half] = jnp.dot(probs, with_ones(cand[1, r : r + half]), preferred_element_type=F32)
        row_max[h, r : r + half] = jnp.broadcast_to(top, (half, hd))

    ahead(pairs, suffix_scores, suffix_rest)

    def absorb(s, h, r, values, last):
        old = row_max[h, r : r + half]
        new = jnp.maximum(old, jnp.max(s, axis=1, keepdims=True))
        shrink = jnp.exp2(old - new)
        probs = jnp.exp2(s - new[:, :1]).astype(BF)
        added = jnp.dot(probs, with_ones(values), preferred_element_type=F32)
        result = acc[h, r : r + half] * jnp.concatenate([shrink, shrink], axis=1) + added
        if last:
            att[0, core, h, r : r + half] = (result[:, :hd] / result[:, hd:]).astype(BF)
        else:
            acc[h, r : r + half] = result
            row_max[h, r : r + half] = new

    def keys_of(kind, pieces):
        parts = [kv[kind, slot, c * rows1 : (c + 1) * rows1] for slot, c in pieces]
        return jnp.concatenate(parts, axis=0) if len(parts) > 1 else parts[0]

    def attend(units):
        ahead(
            units,
            lambda h, r, pieces, last: scores(h, r, keys_of(0, pieces)),
            lambda s, h, r, pieces, last: absorb(s, h, r, keys_of(1, pieces), last),
        )

    wide = total.shape[1]

    def project(slot, pair, first=False):
        dz = (0, 0, 1, 3, 2, 1, 3, 2)[slot]
        dx = (0, 1, 0, 0, 0, 1, 1, 1)[slot]
        group = lax.rem(z + dz, 4) * 2 + lax.rem(x_lo + dx, 2)
        base = group * (2 * heads * hd) + pair * 2 * hd
        pieces, sides = [], []
        for k in (0, 1):
            pieces += [att[slot, k, 2 * pair], att[slot, k, 2 * pair + 1]]
            start = pl.multiple_of(base + k * heads * hd, 2 * hd)
            sides.append(weights[pl.ds(start, 2 * hd), :])
        product = jnp.dot(
            jnp.concatenate(pieces, axis=1), jnp.concatenate(sides, axis=0), preferred_element_type=F32
        )
        total[...] = product if first else total[...] + product

    local[0].wait()
    here, left, projected = set(), [8 * CHUNKS1] * heads, 0
    for step in SCHEDULE:
        if step[0] == ARRIVE:
            on_arrival(*step[1:])
        elif step[0] == ATTEND:
            units = []
            for h, pieces in step[1:]:
                for piece in pieces:
                    if piece not in here:
                        here.add(piece)
                        shared(1, *piece)
                left[h] -= len(pieces)
                units += [(h, r, pieces, left[h] == 0) for r in (0, half)]
            attend(units)
        elif step[0] == LAUNCH:
            own(2, step[1])
        else:
            slot, pair = step[1:]
            shared(2, slot, 2 * pair)
            shared(2, slot, 2 * pair + 1)
            if projected == 0:
                local[3].wait()
            project(slot, pair, projected == 0)
            projected += 1
    out_ref[...] = total[...].astype(out_ref.dtype)

    cand_copy.wait_send()
    for copy in sent:
        copy.wait_send()


def body(queries, prefix_kv, cand_kv, lengths, out_weight):
    tokens, width = queries.shape
    hd = prefix_kv.shape[2]
    heads = width // hd
    positions = prefix_kv.shape[1]
    any_ = pl.BlockSpec(memory_space=pl.ANY)
    args = [
        pltpu.with_memory_space_constraint(a, pltpu.HBM)
        for a in (lengths, queries, prefix_kv, cand_kv, out_weight)
    ]
    dma = pltpu.SemaphoreType.DMA
    return pl.pallas_call(
        attend_kernel,
        out_shape=jax.ShapeDtypeStruct((tokens, out_weight.shape[1]), BF),
        in_specs=[any_] * 5,
        out_specs=pl.BlockSpec(memory_space=pltpu.VMEM),
        scratch_shapes=[
            pltpu.VMEM((2, 8, positions, hd), BF),
            pltpu.VMEM((2, tokens, hd), BF),
            pltpu.VMEM((tokens, width), BF),
            pltpu.VMEM((heads, tokens, 2 * hd), BF),
            pltpu.VMEM(out_weight.shape, BF),
            pltpu.VMEM((heads, tokens, 2 * hd), F32),
            pltpu.VMEM((heads, tokens, hd), F32),
            pltpu.VMEM((8, 2, heads, tokens, hd), BF),
            pltpu.VMEM((tokens, out_weight.shape[1]), F32),
            pltpu.SMEM(lengths.shape, jnp.int32),
            dma((5,)),
            dma((2,)),
            dma((KINDS, CHUNKS1)),
            dma((8, CHUNKS1)),
            dma((8, CHUNKS1)),
            dma((KINDS, heads)),
            dma((8, heads)),
            dma((8, heads)),
        ],
        compiler_params=pltpu.CompilerParams(
            collective_id=0, has_side_effects=True, vmem_limit_bytes=48 * 1024 * 1024
        ),
        name="attend",
    )(*args)


def solution(mesh):
    placed = (
        P("ctx", "head"),
        P("head", "ctx", None),
        P("head", "ctx", None),
        P("ctx"),
        P(None, "head"),
    )
    return jax.shard_map(
        body, mesh=mesh, in_specs=placed, out_specs=P("ctx", "head"), check_vma=False
    )
```

```python
import functools
import math

import jax
import jax.numpy as jnp
from jax import lax
from jax.experimental import pallas as pl
from jax.experimental.pallas import tpu as pltpu
from jax.sharding import PartitionSpec as P

MESH = pl.DeviceIdType.MESH
BF = jnp.bfloat16
F32 = jnp.float32
NEG_FILL = -1e30
NT = (((1,), (1,)), ((), ()))

FORWARD, BACK, OVER = 0, 1, 2
KINDS = 15
CHUNKS1 = 2
ARRIVE, ATTEND, LAUNCH, PROJECT = range(4)
TURNED = 2
SCHEDULE = (
    (ARRIVE, 1, 2, 0),
    (ATTEND, (0, ((0, 1),)), (1, ((0, 0), (0, 1))), (2, ((0, 0),))),
    (ARRIVE, 1, 3, 0),
    (ARRIVE, 1, 2, 1),
    (ARRIVE, 1, 3, 1),
    (ARRIVE, 1, 1, 0),
    (ARRIVE, 1, 1, 1),
    (ATTEND, (3, ((0, 1), (3, 0))), (2, ((2, 0), (3, 0))), (0, ((0, 0),))),
    (ARRIVE, 1, 4, 0),
    (ATTEND, (0, ((1, 0), (1, 1), (2, 0), (2, 1))), (3, ((0, 0), (2, 0), (2, 1))), (2, ((2, 1),))),
    (ARRIVE, 1, 4, 1),
    (ARRIVE, 1, 5, 0),
    (ATTEND, (3, ((1, 0), (1, 1), (4, 0))), (0, ((3, 0), (3, 1), (4, 0))), (2, ((4, 0),)), (1, ((1, 0),))),
    (ARRIVE, 1, 6, 0),
    (ARRIVE, 1, 5, 1),
    (ARRIVE, 1, 7, 0),
    (ATTEND, (3, ((3, 1), (5, 0))), (2, ((0, 1), (3, 1), (5, 0))), (0, ((5, 0),))),
    (ARRIVE, 1, 6, 1),
    (ARRIVE, 1, 7, 1),
    (ATTEND, (3, ((4, 1), (5, 1), (6, 0), (7, 0))), (0, ((4, 1), (6, 0))), (2, ((1, 1),))),
    (ATTEND, (3, ((6, 1), (7, 1)))),
    (LAUNCH, 3),
    (ATTEND, (0, ((5, 1), (6, 1), (7, 0), (7, 1)))),
    (LAUNCH, 0),
    (ATTEND, (2, ((1, 0), (4, 1), (5, 1), (6, 0), (6, 1), (7, 0), (7, 1)))),
    (LAUNCH, 2),
    (ATTEND, (1, ((1, 1), (2, 0), (2, 1), (3, 0), (3, 1), (4, 0), (4, 1), (5, 0), (5, 1), (6, 0), (6, 1), (7, 0), (7, 1)))),
    (LAUNCH, 1),
    (ARRIVE, 2, 2, 0),
    (ARRIVE, 2, 3, 2),
    (ARRIVE, 2, 2, 2),
    (ARRIVE, 2, 3, 3),
    (ARRIVE, 2, 3, 1),
    (PROJECT, 3, 1),
    (ARRIVE, 2, 1, 3),
    (ARRIVE, 2, 1, 2),
    (ARRIVE, 2, 3, 0),
    (ARRIVE, 2, 4, 3),
    (ARRIVE, 2, 1, 0),
    (ARRIVE, 2, 1, 1),
    (PROJECT, 0, 1),
    (ARRIVE, 2, 4, 2),
    (ARRIVE, 2, 4, 0),
    (ARRIVE, 2, 4, 1),
    (ARRIVE, 2, 7, 3),
    (ARRIVE, 2, 2, 1),
    (ARRIVE, 2, 5, 2),
    (ARRIVE, 2, 6, 3),
    (ARRIVE, 2, 2, 3),
    (PROJECT, 1, 0),
    (PROJECT, 0, 0),
    (PROJECT, 4, 0),
    (PROJECT, 4, 1),
    (ARRIVE, 2, 6, 2),
    (PROJECT, 2, 0),
    (ARRIVE, 2, 6, 0),
    (PROJECT, 3, 0),
    (ARRIVE, 2, 5, 0),
    (ARRIVE, 2, 5, 3),
    (PROJECT, 6, 1),
    (PROJECT, 2, 1),
    (ARRIVE, 2, 6, 1),
    (PROJECT, 1, 1),
    (ARRIVE, 2, 5, 1),
    (ARRIVE, 2, 7, 0),
    (ARRIVE, 2, 7, 1),
    (PROJECT, 5, 1),
    (PROJECT, 6, 0),
    (PROJECT, 5, 0),
    (ARRIVE, 2, 7, 2),
    (PROJECT, 7, 0),
    (PROJECT, 7, 1),
)


def attend_kernel(
    lengths_hbm, q_hbm, pre_hbm, cand_hbm, w_hbm, out_ref,
    kv, cand, q_raw, q_two, weights, acc, row_max, att, total,
    lengths_ref, local_sem, cand_sem, s1, r1, b1, s2, r2, b2,
):
    ctx, head = lax.axis_index("ctx"), lax.axis_index("head")
    y, x_hi = ctx // 2, ctx % 2
    z, x_lo, core = head // 4, (head // 2) % 2, head % 2

    def ring1(d):
        return (lax.rem(y + d, 4) * 2 + x_hi, head)

    def ring2(d):
        return (ctx, lax.rem(z + d, 4) * 4 + x_lo * 2 + core)

    over1 = (y * 2 + 1 - x_hi, head)
    over2 = (ctx, z * 4 + (1 - x_lo) * 2 + core)
    sibling = (ctx, z * 4 + x_lo * 2 + 1 - core)
    near1 = {FORWARD: ring1(1), BACK: ring1(3), OVER: over1}
    near2 = {FORWARD: ring2(1), BACK: ring2(3), OVER: over2}

    barrier = pltpu.get_barrier_semaphore()
    others = [*near1.values(), *near2.values(), sibling]
    for other in others:
        pl.semaphore_signal(barrier, inc=1, device_id=other, device_id_type=MESH)

    local = [
        pltpu.make_async_copy(pre_hbm.at[0], kv.at[core, 0], local_sem.at[0]),
        pltpu.make_async_copy(cand_hbm.at[0], cand.at[core], local_sem.at[1]),
        pltpu.make_async_copy(q_hbm, q_raw, local_sem.at[2]),
        pltpu.make_async_copy(w_hbm, weights, local_sem.at[3]),
        pltpu.make_async_copy(lengths_hbm, lengths_ref, local_sem.at[4]),
    ]
    for copy in local[:3] + local[4:]:
        copy.start()

    def remote(src, dst, send, recv, device):
        return pltpu.make_async_remote_copy(
            src_ref=src, dst_ref=dst, send_sem=send, recv_sem=recv, device_id=device, device_id_type=MESH
        )

    rows1 = kv.shape[2] // CHUNKS1

    def piece1(slot, c):
        return kv.at[core, slot, pl.ds(c * rows1, rows1)]

    def piece2(slot, c):
        return att.at[slot, core, c]

    sent = []

    def send(phase, src_slot, dst_slot, c, kind, device):
        piece, ss, rr = (piece1, s1, r1) if phase == 1 else (piece2, s2, r2)
        src = piece(src_slot, c)
        if phase == 1 and src_slot == 0:
            src = pre_hbm.at[0, pl.ds(c * rows1, rows1)]
        copy = remote(src, piece(dst_slot, c), ss.at[kind, c], rr.at[dst_slot, c], device)
        copy.start()
        sent.append(copy)

    def share(phase, slot, c):
        piece, ss, bb = (piece1, s1, b1) if phase == 1 else (piece2, s2, b2)
        src = piece(slot, c)
        if phase == 1 and slot == 0:
            src = pre_hbm.at[0, pl.ds(c * rows1, rows1)]
        copy = remote(src, piece(slot, c), ss.at[6 + slot, c], bb.at[slot, c], sibling)
        copy.start()
        sent.append(copy)

    def arrived(phase, slot, c):
        piece, rr = (piece1, r1) if phase == 1 else (piece2, r2)
        ref = piece(slot, c)
        remote(ref, ref, rr.at[slot, c], rr.at[slot, c], sibling).wait_recv()

    def shared(phase, slot, c):
        if phase == 1:
            ref, bb = kv.at[1 - core, slot, pl.ds(c * rows1, rows1)], b1
        else:
            ref, bb = att.at[slot, 1 - core, c], b2
        remote(ref, ref, bb.at[slot, c], bb.at[slot, c], sibling).wait_recv()

    def near(phase):
        return near1 if phase == 1 else near2

    def own(phase, c):
        n = near(phase)
        send(phase, 0, 1, c, 0, n[OVER])
        send(phase, 0, 3, c, 1, n[FORWARD])
        send(phase, 0, 2, c, 2, n[BACK])
        share(phase, 0, c)

    def on_arrival(phase, slot, c):
        n = near(phase)
        arrived(phase, slot, c)
        turned = phase == 2 and c == TURNED
        if slot == 1 and not turned:
            send(phase, 1, 6, c, 4, n[FORWARD])
            send(phase, 1, 5, c, 5, n[BACK])
        if slot in (2, 3) and turned:
            send(phase, slot, slot + 3, c, 2 + slot, n[OVER])
        if slot == 5 + c % 2 and turned:
            send(phase, slot, 7, c, 14, n[FORWARD if c % 2 else BACK])
        if slot == 2 and c % 2 == 0:
            send(phase, 2, 4, c, 3, n[BACK])
        if slot == 3 and c % 2 == 1:
            send(phase, 3, 4, c, 3, n[FORWARD])
        if slot == 4 and not turned:
            send(phase, 4, 7, c, 14, n[OVER])
        share(phase, slot, c)

    heads = q_two.shape[0]
    hd = kv.shape[3]
    factor = hd ** (-0.5) * math.log2(math.e)
    local[2].wait()
    for h in range(heads):
        scaled = q_raw[:, h * hd : (h + 1) * hd].astype(F32) * factor
        high = scaled.astype(BF)
        q_two[h, :, :hd] = high
        q_two[h, :, hd:] = (scaled - high.astype(F32)).astype(BF)

    pl.semaphore_wait(barrier, len(others))

    cand_copy = remote(cand_hbm.at[0], cand.at[core], cand_sem.at[0], cand_sem.at[1], sibling)
    cand_copy.start()
    for c in range(CHUNKS1):
        own(1, c)
    local[3].start()

    tokens = q_two.shape[1]
    half = tokens // 2
    pairs = [(h, r) for h in range(heads) for r in (0, half)]

    def twice(k):
        return jnp.concatenate([k, k], axis=1)

    def with_ones(v):
        return jnp.concatenate([v, jnp.ones_like(v)], axis=1)

    def scores(h, r, keys):
        return lax.dot_general(q_two[h, r : r + half], twice(keys), NT, preferred_element_type=F32)

    def ahead(units, first, second):
        held = first(*units[0])
        for i, unit in enumerate(units):
            following = first(*units[i + 1]) if i + 1 < len(units) else None
            second(held, *unit)
            held = following

    local[1].wait()
    local[4].wait()
    remote(cand.at[1 - core], cand.at[1 - core], cand_sem.at[0], cand_sem.at[1], sibling).wait_recv()
    slots = tokens // lengths_ref.shape[0]
    per = half // slots
    row = lax.broadcasted_iota(jnp.int32, (half, half), 0)
    col = lax.broadcasted_iota(jnp.int32, (half, half), 1)
    row_cand, col_cand = row // slots, col // slots
    causal = (row_cand == col_cand) & (col <= row)
    masks = []
    for part in range(2):
        limit = jnp.zeros((half, half), jnp.int32)
        for j in range(per):
            limit = jnp.where(col_cand == j, lengths_ref[part * per + j] + j * slots, limit)
        masks.append(causal & (col < limit))

    def suffix_scores(h, r):
        return jnp.where(masks[r // half], scores(h, r, cand[0, r : r + half]), NEG_FILL)

    def suffix_rest(s, h, r):
        top = jnp.max(s, axis=1, keepdims=True)
        probs = jnp.exp2(s - top).astype(BF)
        acc[h, r : r + half] = jnp.dot(probs, with_ones(cand[1, r : r + half]), preferred_element_type=F32)
        row_max[h, r : r + half] = jnp.broadcast_to(top, (half, hd))

    ahead(pairs, suffix_scores, suffix_rest)

    def absorb(s, h, r, values, last):
        old = row_max[h, r : r + half]
        new = jnp.maximum(old, jnp.max(s, axis=1, keepdims=True))
        shrink = jnp.exp2(old - new)
        probs = jnp.exp2(s - new[:, :1]).astype(BF)
        added = jnp.dot(probs, with_ones(values), preferred_element_type=F32)
        result = acc[h, r : r + half] * jnp.concatenate([shrink, shrink], axis=1) + added
        if last:
            att[0, core, h, r : r + half] = (result[:, :hd] / result[:, hd:]).astype(BF)
        else:
            acc[h, r : r + half] = result
            row_max[h, r : r + half] = new

    def keys_of(kind, pieces):
        parts = [kv[kind, slot, c * rows1 : (c + 1) * rows1] for slot, c in pieces]
        return jnp.concatenate(parts, axis=0) if len(parts) > 1 else parts[0]

    def attend(units):
        ahead(
            units,
            lambda h, r, pieces, last: scores(h, r, keys_of(0, pieces)),
            lambda s, h, r, pieces, last: absorb(s, h, r, keys_of(1, pieces), last),
        )

    wide = total.shape[1]

    def project(slot, pair, first=False):
        dz = (0, 0, 1, 3, 2, 1, 3, 2)[slot]
        dx = (0, 1, 0, 0, 0, 1, 1, 1)[slot]
        group = lax.rem(z + dz, 4) * 2 + lax.rem(x_lo + dx, 2)
        base = group * (2 * heads * hd) + pair * 2 * hd
        pieces, sides = [], []
        for k in (0, 1):
            pieces += [att[slot, k, 2 * pair], att[slot, k, 2 * pair + 1]]
            start = pl.multiple_of(base + k * heads * hd, 2 * hd)
            sides.append(weights[pl.ds(start, 2 * hd), :])
        product = jnp.dot(
            jnp.concatenate(pieces, axis=1), jnp.concatenate(sides, axis=0), preferred_element_type=F32
        )
        total[...] = product if first else total[...] + product

    local[0].wait()
    here, left, projected = set(), [8 * CHUNKS1] * heads, 0
    for step in SCHEDULE:
        if step[0] == ARRIVE:
            on_arrival(*step[1:])
        elif step[0] == ATTEND:
            units = []
            for h, pieces in step[1:]:
                for piece in pieces:
                    if piece not in here:
                        here.add(piece)
                        shared(1, *piece)
                left[h] -= len(pieces)
                units += [(h, r, pieces, left[h] == 0) for r in (0, half)]
            attend(units)
        elif step[0] == LAUNCH:
            own(2, step[1])
        else:
            slot, pair = step[1:]
            shared(2, slot, 2 * pair)
            shared(2, slot, 2 * pair + 1)
            if projected == 0:
                local[3].wait()
            project(slot, pair, projected == 0)
            projected += 1
    out_ref[...] = total[...].astype(out_ref.dtype)

    cand_copy.wait_send()
    for copy in sent:
        copy.wait_send()


def body(queries, prefix_kv, cand_kv, lengths, out_weight):
    tokens, width = queries.shape
    hd = prefix_kv.shape[2]
    heads = width // hd
    positions = prefix_kv.shape[1]
    any_ = pl.BlockSpec(memory_space=pl.ANY)
    args = [
        pltpu.with_memory_space_constraint(a, pltpu.HBM)
        for a in (lengths, queries, prefix_kv, cand_kv, out_weight)
    ]
    dma = pltpu.SemaphoreType.DMA
    return pl.pallas_call(
        attend_kernel,
        out_shape=jax.ShapeDtypeStruct((tokens, out_weight.shape[1]), BF),
        in_specs=[any_] * 5,
        out_specs=pl.BlockSpec(memory_space=pltpu.VMEM),
        scratch_shapes=[
            pltpu.VMEM((2, 8, positions, hd), BF),
            pltpu.VMEM((2, tokens, hd), BF),
            pltpu.VMEM((tokens, width), BF),
            pltpu.VMEM((heads, tokens, 2 * hd), BF),
            pltpu.VMEM(out_weight.shape, BF),
            pltpu.VMEM((heads, tokens, 2 * hd), F32),
            pltpu.VMEM((heads, tokens, hd), F32),
            pltpu.VMEM((8, 2, heads, tokens, hd), BF),
            pltpu.VMEM((tokens, out_weight.shape[1]), F32),
            pltpu.SMEM(lengths.shape, jnp.int32),
            dma((5,)),
            dma((2,)),
            dma((KINDS, CHUNKS1)),
            dma((8, CHUNKS1)),
            dma((8, CHUNKS1)),
            dma((KINDS, heads)),
            dma((8, heads)),
            dma((8, heads)),
        ],
        compiler_params=pltpu.CompilerParams(
            collective_id=0, has_side_effects=True, vmem_limit_bytes=48 * 1024 * 1024
        ),
        name="attend",
    )(*args)


def solution(mesh):
    placed = (
        P("ctx", "head"),
        P("head", "ctx", None),
        P("head", "ctx", None),
        P("ctx"),
        P(None, "head"),
    )
    return jax.shard_map(
        body, mesh=mesh, in_specs=placed, out_specs=P("ctx", "head"), check_vma=False
    )
```
